256 devices in a mesh: var: 8 (over x, y_lo), space: 32 (over y_hi, z, core).
Axes of the slice: x: 4, y: 4 (y_hi: 2, y_lo: 2; y = y_hi * 2 + y_lo), z: 8, core: 2. Of those that a mesh axis runs over, the one named last changes fastest.
Arguments:
- order_field: float32 [128, 3, 1024, 1024], P('var', None, 'space'), may hold values from -1 to 1
- solute: float32 [3, 1024, 1024], P(None, 'space'), may hold values from 0.05 to 0.95
- active: int32 [32, 64], P(None, 'var'), may hold values from 0 to 1, as said below
Outputs:
- new_order: float32 [128, 3, 1024, 1024], P('var', None, 'space')
- new_solute: float32 [3, 1024, 1024], P(None, 'space')
The draws below stay inside these ranges and needn't reach their ends.
Inputs may be any that keep to these rules, and one draw needn't show every extreme that they name: On every tile, each index of var holds at least 1 and at most 4 active blocks among its 8; in every draw some tile and index of var hold exactly 4.
All inputs are finite; a program needn't handle non-finite values.
Results may differ from the reference program's by a relative error of at most 0.00005.
Values sent between devices are 32-bit elements; how exact they have to be, the bound alone decides.
A program may use at most 128 MiB of HBM per device.

```python
import jax
import jax.numpy as jnp
from jax import lax

P_SIZE = 128
BV = 2
ZP = 3
NY = 1024
ROWS = 32
NX = 1024
TILES = 32
BLOCKS = 64
BPD = 8
KMAX = 4


def draw_active(key, part):
    key = jax.random.fold_in(key, 11)
    first_key, second_key, third_key = jax.random.split(key, 3)
    groups = BLOCKS // BPD
    counts = jax.random.randint(first_key, (TILES * groups,), 1, KMAX + 1)
    chosen = jax.random.randint(second_key, (), 0, TILES * groups)
    counts = jnp.where(jnp.arange(TILES * groups) == chosen, KMAX, counts).reshape(TILES, groups)
    scores = jax.random.randint(third_key, (TILES, groups, BPD), 0, 1048576)
    scores = scores * BPD + jnp.arange(BPD, dtype=jnp.int32)[None, None, :]
    order_rank = jnp.argsort(jnp.argsort(scores, axis=-1), axis=-1)
    chosen_blocks = (order_rank < counts[:, :, None]).astype(jnp.int32)
    return chosen_blocks.reshape(TILES, groups * BPD)


def block_levels(stream_key, extent, shards, least, high):
    def one(dim, blocks):
        draws = jax.random.uniform(jax.random.fold_in(jax.random.fold_in(stream_key, 6), dim), (blocks,), jnp.float32, least / len(shards), high / len(shards))
        return jnp.repeat(jnp.exp(draws), extent[dim] // blocks).reshape((-1,) + (1,) * (len(extent) - dim - 1))

    factor_of = one(*shards[0])
    for cut in shards[1:]:
        factor_of = factor_of * one(*cut)
    return factor_of


def setup_inputs(seed: int = 0) -> dict:
    key_list = jax.random.split(jax.random.key(seed), 4)
    order_field = jnp.clip(jax.random.uniform(key_list[0], (P_SIZE, ZP, NX, NY), jnp.float32, -1.0, 1.0) * block_levels(key_list[0], (P_SIZE, ZP, NX, NY), ((0, 8), (2, 32)), -0.4, 0.0), -1.0, 1.0)
    solute = jnp.clip(0.05 + 0.9 * jax.random.uniform(key_list[1], (ZP, NX, NY), jnp.float32) ** block_levels(key_list[1], (ZP, NX, NY), ((1, 32),), -0.2, 0.2), 0.05, 0.95)
    active = draw_active(jax.random.fold_in(key_list[3], 71), 0)
    return {"order_field": order_field, "solute": solute, "active": active}


def laplace(field):
    above_plane = jnp.concatenate([field[1:], field[-1:]], axis=0)
    below_plane = jnp.concatenate([field[:1], field[:-1]], axis=0)
    summed = jnp.roll(field, 1, axis=-2) + jnp.roll(field, -1, axis=-2)
    summed = summed + jnp.roll(field, 1, axis=-1) + jnp.roll(field, -1, axis=-1)
    return summed + above_plane + below_plane - 6.0 * field


def reference(order_field, solute, active):
    weights = jnp.repeat(jnp.repeat(active.T.astype(jnp.float32), BV, axis=0), ROWS, axis=1)

    def add_square(carried, inputs):
        variant_slab, row_weight = inputs
        live_eta = variant_slab * row_weight[None, :, None]
        return carried + live_eta * live_eta, None

    sum_squares, _ = lax.scan(add_square, jnp.zeros(solute.shape, jnp.float32), (order_field, weights))
    shifted = solute - 0.05

    def update_one(inputs):
        variant_slab, row_weight = inputs
        weight_grid = row_weight[None, :, None]
        live_eta = variant_slab * weight_grid
        change = -0.5 * shifted * shifted * live_eta + live_eta * live_eta * live_eta
        change = change + 0.4 * live_eta * (sum_squares - live_eta * live_eta) - 2.0 * laplace(live_eta)
        return (live_eta - 0.01 * change) * weight_grid

    new_order = lax.map(update_one, (order_field, weights))
    middle = solute - 0.5
    upper_gap = solute - 0.95
    potential = -2.0 * middle + 9.88 * middle ** 3 + 2.0 * shifted ** 3 + 2.0 * upper_gap ** 3
    potential = potential - 0.5 * shifted * sum_squares - laplace(solute)
    new_solute = solute + 0.01 * laplace(potential)
    return new_order, new_solute
```

```python
import functools

import jax
import jax.numpy as jnp
from jax import lax
from jax.experimental import pallas as pl
from jax.experimental.pallas import tpu as pltpu
from jax.sharding import PartitionSpec as P

MESH = pl.DeviceIdType.MESH
F32 = jnp.float32
PLANES, ROWS, COLS, LANES = 3, 32, 1024, 128
VARIANTS, BLOCKS, BV, KMAX = 16, 8, 2, 4
SLOTS = KMAX * BV
GROUP, TILES = 8, 32
PEERS = ((1, 0), (0, 1), (3, 0), (2, 1), (1, 1), (2, 0), (3, 1))


def tile_blocks(active_ref, tile):
    flags = [active_ref[tile, b] for b in range(BLOCKS)]
    blocks = [jnp.int32(0)] * KMAX
    rank = jnp.int32(0)
    for b in range(BLOCKS):
        for k in range(KMAX):
            hit = jnp.where(rank == k, flags[b], 0)
            blocks[k] = blocks[k] + b * hit
        rank = rank + flags[b]
    weights = [jnp.where(rank > k, 1.0, 0.0).astype(F32) for k in range(KMAX)]
    return blocks, weights


def rows_sum(value):
    row = lax.broadcasted_iota(jnp.int32, value.shape, 0)
    before = jnp.where(row == 0, 0.0, pltpu.roll(value, 1, 0))
    after = jnp.where(row == value.shape[0] - 1, 0.0, pltpu.roll(value, value.shape[0] - 1, 0))
    return before + after


def cells_sum(value):
    return pltpu.roll(value, 1, 1) + pltpu.roll(value, value.shape[1] - 1, 1)


def plane_sum(planes, z):
    return planes[min(z + 1, PLANES - 1)] + planes[max(z - 1, 0)]


def bulk(value):
    middle = value - 0.5
    shifted = value - 0.05
    gap = value - 0.95
    return (-2.0 * middle + 9.88 * middle * middle * middle
            + 2.0 * shifted * shifted * shifted + 2.0 * gap * gap * gap)


def exchange(order, solute, active, base, slope, squares, quiet, held, edge_quiet, edge_held, edge_squares,
             field0, field1, field2, part, landed, row_out, row_in, edge_out,
             load_sem, solute_sem, row_send, row_recv, sum_send, sum_recv, all_send, all_recv, edge_send, edge_recv):
    v, tile = lax.axis_index("var"), lax.axis_index("space")
    x, y = v // 2, v % 2
    below, above = lax.rem(tile + TILES - 1, TILES), lax.rem(tile + 1, TILES)
    sides = (below, above)
    peers = [lax.rem(x + dx, 4) * 2 + (y + dy - 2 * y * dy) for dx, dy in PEERS]
    fields = (field0, field1, field2)

    loads = [pltpu.make_async_copy(order.at[:, z], fields[z], load_sem.at[z]) for z in range(PLANES)]
    for copy in loads:
        copy.start()
    solute_load = pltpu.make_async_copy(solute, held, solute_sem)
    solute_load.start()

    barrier = pltpu.get_barrier_semaphore()
    for peer in peers:
        pl.semaphore_signal(barrier, inc=1, device_id=(peer, tile), device_id_type=MESH)
    for side in sides:
        for d in range(GROUP):
            pl.semaphore_signal(barrier, inc=1, device_id=(lax.rem(v + d, GROUP), side), device_id_type=MESH)

    blocks, weights = tile_blocks(active, tile)
    side_blocks = [tile_blocks(active, side)[0] for side in sides]

    waiting = []
    sums = []
    for z in range(PLANES):
        loads[z].wait()
        total = jnp.zeros((ROWS, COLS), F32)
        for k in range(KMAX):
            for i in range(BV):
                one = fields[z][blocks[k] * BV + i]
                total = total + one * one * weights[k]
        for p in range(GROUP):
            part[z, p] = total[:, p * LANES:(p + 1) * LANES]
        if z == 0:
            pl.semaphore_wait(barrier, GROUP - 1 + 2 * GROUP)
        for d, peer in enumerate(peers):
            copy = pltpu.make_async_remote_copy(
                part.at[z, peer], landed.at[z, d], sum_send.at[z, d], sum_recv.at[z, d],
                device_id=(peer, tile), device_id_type=MESH)
            copy.start()
            sums.append(copy)

    solute_load.wait()
    row_copies = []
    for s, side in enumerate(sides):
        edge = 0 if s == 0 else ROWS - 1
        for k in range(KMAX):
            block = side_blocks[s][k]
            weight = active[tile, block].astype(F32)
            for i in range(BV):
                slot = k * BV + i
                for z in range(PLANES):
                    row_out[s, z * SLOTS + slot:z * SLOTS + slot + 1, :] = (
                        fields[z][block * BV + i, edge:edge + 1, :] * weight)
        first = 0 if s == 0 else ROWS - 2
        for z in range(PLANES):
            row_out[s, 24 + 2 * z:26 + 2 * z, :] = held[z, first:first + 2, :]
        row_out[s, 30:32, :] = jnp.zeros((2, COLS), F32)
        copy = pltpu.make_async_remote_copy(
            row_out.at[s], row_in.at[1 - s], row_send.at[s], row_recv.at[1 - s],
            device_id=(v, side), device_id_type=MESH)
        copy.start()
        row_copies.append(copy)

    def local(slot, block, weight, i):
        ones = [fields[z][block * BV + i] for z in range(PLANES)]
        for z in range(PLANES):
            one = ones[z]
            shifted = held[z] - 0.05
            near = rows_sum(one) + cells_sum(one) + plane_sum(ones, z)
            value = one * (0.88 + 0.005 * (shifted * shifted) - 0.006 * (one * one)) + 0.02 * near
            base[slot, z] = value * weight
            slope[slot, z] = one * (0.004 * weight)

    def reduce_plane(z):
        total = part[z, v]
        for d in range(GROUP - 1):
            sums[z * (GROUP - 1) + d].wait_recv()
            total = total + landed[z, d]
        squares[z, v] = total
        edge_out[0, z:z + 1, :] = total[0:1, :]
        edge_out[1, z:z + 1, :] = total[ROWS - 1:ROWS, :]
        for d, peer in enumerate(peers):
            copy = pltpu.make_async_remote_copy(
                squares.at[z, v], squares.at[z, v], all_send.at[z, d], all_recv.at[z, d],
                device_id=(peer, tile), device_id_type=MESH)
            copy.start()
            gathers.append(copy)

    gathers = []
    edge_out[0, 3:8, :] = jnp.zeros((5, LANES), F32)
    edge_out[1, 3:8, :] = jnp.zeros((5, LANES), F32)
    for k in range(KMAX):
        for i in range(BV):
            local(k * BV + i, blocks[k], weights[k], i)
    reduce_plane(0)
    solutes = [held[z] for z in range(PLANES)]
    for z in range(PLANES):
        value = solutes[z]
        quiet[z] = bulk(value) + 6.0 * value - rows_sum(value) - cells_sum(value) - plane_sum(solutes, z)
    reduce_plane(1)
    reduce_plane(2)
    edges = []
    for s, side in enumerate(sides):
        for d in range(GROUP):
            copy = pltpu.make_async_remote_copy(
                edge_out.at[s], edge_squares.at[1 - s, v], edge_send.at[s, d], edge_recv.at[1 - s, d],
                device_id=(lax.rem(v + d, GROUP), side), device_id_type=MESH)
            copy.start()
            edges.append(copy)

    for copy in row_copies:
        copy.wait_recv()
    for s in range(2):
        row = 0 if s == 0 else ROWS - 1
        for k in range(KMAX):
            for i in range(BV):
                slot = k * BV + i
                for z in range(PLANES):
                    base[slot, z, row:row + 1, :] = base[slot, z, row:row + 1, :] + (
                        row_in[s, z * SLOTS + slot:z * SLOTS + slot + 1, :] * (0.02 * weights[k]))
        near_row, far_row = (1, 0) if s == 0 else (0, 1)
        nears = [row_in[s, 24 + 2 * z + near_row:25 + 2 * z + near_row, :] for z in range(PLANES)]
        for z in range(PLANES):
            far = row_in[s, 24 + 2 * z + far_row:25 + 2 * z + far_row, :]
            quiet[z, row:row + 1, :] = quiet[z, row:row + 1, :] - nears[z]
            around = far + held[z, row:row + 1, :] + cells_sum(nears[z]) + plane_sum(nears, z)
            edge_quiet[s, z:z + 1, :] = bulk(nears[z]) + 6.0 * nears[z] - around
            edge_held[s, z:z + 1, :] = nears[z]
        edge_quiet[s, 3:8, :] = jnp.zeros((5, COLS), F32)
        edge_held[s, 3:8, :] = jnp.zeros((5, COLS), F32)

    for copy in gathers:
        copy.wait_recv()
    for copy in edges:
        copy.wait_recv()
    for copy in sums + gathers + edges + row_copies:
        copy.wait_send()


def finish(active, base, slope, squares, quiet, held, edge_quiet, edge_held, edge_squares, new_order, new_solute,
           blank, stage, solute_stage, order_sem, solute_sem):
    tile = lax.axis_index("space")
    blank[...] = jnp.zeros(blank.shape, F32)
    flags = [active[tile, b] for b in range(BLOCKS)]
    for b in range(BLOCKS):
        @pl.when(flags[b] == 0)
        def _():
            pltpu.make_async_copy(blank, new_order.at[pl.ds(b * BV, BV)], order_sem.at[b]).start()
    rank = jnp.int32(0)
    for b in range(BLOCKS):
        @pl.when(flags[b] != 0)
        def _(rank=rank):
            for i in range(BV):
                for z in range(PLANES):
                    for p in range(GROUP):
                        cut = slice(p * LANES, (p + 1) * LANES)
                        stage[rank, i, z, :, cut] = (
                            base[rank * BV + i, z, :, cut] - slope[rank * BV + i, z, :, cut] * squares[z, p])
            pltpu.make_async_copy(stage.at[rank], new_order.at[pl.ds(b * BV, BV)], order_sem.at[b]).start()
        rank = rank + flags[b]

    pots = []
    for z in range(PLANES):
        total = jnp.concatenate([squares[z, p] for p in range(GROUP)], axis=1)
        pots.append(quiet[z] - 0.5 * (held[z] - 0.05) * total)
    ends = []
    for s in range(2):
        total = jnp.concatenate([edge_squares[s, p] for p in range(GROUP)], axis=1)
        ends.append(edge_quiet[s] - 0.5 * (edge_held[s] - 0.05) * total)
    row = lax.broadcasted_iota(jnp.int32, (ROWS, COLS), 0)
    for z in range(PLANES):
        value = pots[z]
        before = jnp.where(row == 0, jnp.broadcast_to(ends[0][z:z + 1, :], (ROWS, COLS)), pltpu.roll(value, 1, 0))
        after = jnp.where(row == ROWS - 1, jnp.broadcast_to(ends[1][z:z + 1, :], (ROWS, COLS)),
                          pltpu.roll(value, ROWS - 1, 0))
        lap = before + after + cells_sum(value) + plane_sum(pots, z) - 6.0 * value
        solute_stage[z] = held[z] + 0.01 * lap
    out = pltpu.make_async_copy(solute_stage, new_solute, solute_sem)
    out.start()
    for b in range(BLOCKS):
        pltpu.make_async_copy(blank, new_order.at[pl.ds(b * BV, BV)], order_sem.at[b]).wait()
    out.wait()


def shards(order, solute, active):
    vmem = pl.BlockSpec(memory_space=pltpu.VMEM)
    smem = pl.BlockSpec(memory_space=pltpu.SMEM)
    anywhere = pl.BlockSpec(memory_space=pl.ANY)
    dma = pltpu.SemaphoreType.DMA
    handed = [
        (SLOTS, PLANES, ROWS, COLS),
        (SLOTS, PLANES, ROWS, COLS),
        (PLANES, GROUP, ROWS, LANES),
        (PLANES, ROWS, COLS),
        (PLANES, ROWS, COLS),
        (2, 8, COLS),
        (2, 8, COLS),
        (2, GROUP, 8, LANES),
    ]
    results = pl.pallas_call(
        exchange,
        out_shape=[pltpu.VMEM(shape, F32) for shape in handed],
        in_specs=[anywhere, anywhere, smem],
        out_specs=[vmem] * len(handed),
        scratch_shapes=[
            pltpu.VMEM((VARIANTS, ROWS, COLS), F32),
            pltpu.VMEM((VARIANTS, ROWS, COLS), F32),
            pltpu.VMEM((VARIANTS, ROWS, COLS), F32),
            pltpu.VMEM((PLANES, GROUP, ROWS, LANES), F32),
            pltpu.VMEM((PLANES, GROUP - 1, ROWS, LANES), F32),
            pltpu.VMEM((2, 32, COLS), F32),
            pltpu.VMEM((2, 32, COLS), F32),
            pltpu.VMEM((2, 8, LANES), F32),
            dma((PLANES,)),
            dma,
            dma((2,)),
            dma((2,)),
            dma((PLANES, GROUP - 1)),
            dma((PLANES, GROUP - 1)),
            dma((PLANES, GROUP - 1)),
            dma((PLANES, GROUP - 1)),
            dma((2, GROUP)),
            dma((2, GROUP)),
        ],
        compiler_params=pltpu.CompilerParams(
            collective_id=0, has_side_effects=True, vmem_limit_bytes=32 << 20),
        name="exchange",
    )(order, solute, active)
    return pl.pallas_call(
        finish,
        out_shape=[
            jax.ShapeDtypeStruct(order.shape, F32),
            jax.ShapeDtypeStruct(solute.shape, F32),
        ],
        in_specs=[smem] + [vmem] * len(handed),
        out_specs=[anywhere, anywhere],
        scratch_shapes=[
            pltpu.VMEM((BV, PLANES, ROWS, COLS), F32),
            pltpu.VMEM((KMAX, BV, PLANES, ROWS, COLS), F32),
            pltpu.VMEM((PLANES, ROWS, COLS), F32),
            dma((BLOCKS,)),
            dma,
        ],
        compiler_params=pltpu.CompilerParams(vmem_limit_bytes=32 << 20),
        name="finish",
    )(active, *results)


def solution(mesh):
    return jax.shard_map(
        shards,
        mesh=mesh,
        in_specs=(P("var", None, "space", None), P(None, "space", None), P(None, "var")),
        out_specs=(P("var", None, "space", None), P(None, "space", None)),
        check_vma=False,
    )
```

```python
import functools

import jax
import jax.numpy as jnp
from jax import lax
from jax.experimental import pallas as pl
from jax.experimental.pallas import tpu as pltpu
from jax.sharding import PartitionSpec as P

MESH = pl.DeviceIdType.MESH
F32 = jnp.float32
PLANES, ROWS, COLS, LANES = 3, 32, 1024, 128
VARIANTS, BLOCKS, BV, KMAX = 16, 8, 2, 4
SLOTS = KMAX * BV
GROUP, TILES = 8, 32
SUB, GROUPS = 8, 4
PIECES = (0, 3, 1, 2)
PEERS = ((1, 0), (0, 1), (3, 0), (2, 1), (1, 1), (2, 0), (3, 1))


def tile_blocks(active_ref, tile):
    flags = [active_ref[b, tile] for b in range(BLOCKS)]
    blocks = [jnp.int32(0)] * KMAX
    rank = jnp.int32(0)
    for b in range(BLOCKS):
        for k in range(KMAX):
            hit = jnp.where(rank == k, flags[b], 0)
            blocks[k] = blocks[k] + b * hit
        rank = rank + flags[b]
    weights = [jnp.where(rank > k, 1.0, 0.0).astype(F32) for k in range(KMAX)]
    return blocks, weights


def rows_sum(value):
    row = lax.broadcasted_iota(jnp.int32, value.shape, 0)
    before = jnp.where(row == 0, 0.0, pltpu.roll(value, 1, 0))
    after = jnp.where(row == value.shape[0] - 1, 0.0, pltpu.roll(value, value.shape[0] - 1, 0))
    return before + after


def cells_sum(value):
    return pltpu.roll(value, 1, 1) + pltpu.roll(value, value.shape[1] - 1, 1)


def plane_sum(planes, z):
    return planes[min(z + 1, PLANES - 1)] + planes[max(z - 1, 0)]


def bulk(value):
    middle = value - 0.5
    shifted = value - 0.05
    gap = value - 0.95
    return (-2.0 * middle + 9.88 * middle * middle * middle
            + 2.0 * shifted * shifted * shifted + 2.0 * gap * gap * gap)


def exchange(order, solute, active_hbm, base, slope, squares, quiet, held, edge_quiet, edge_held, edge_squares,
             field0, field1, field2, field3, part, landed, row_out, row_in, edge_out,
             active, active_sem, load_sem, solute_sem, near_sem, row_send, row_recv,
             sum_send, sum_recv, all_send, all_recv, edge_send, edge_recv):
    v, tile = lax.axis_index("var"), lax.axis_index("space")
    x, y = v // 2, v % 2
    below, above = lax.rem(tile + TILES - 1, TILES), lax.rem(tile + 1, TILES)
    sides = (below, above)
    peers = [lax.rem(x + dx, 4) * 2 + (y + dy - 2 * y * dy) for dx, dy in PEERS]
    fields = (field0, field1, field2, field3)

    active_load = pltpu.make_async_copy(active_hbm, active, active_sem)
    active_load.start()
    loads = {}
    for g in PIECES:
        loads[g] = pltpu.make_async_copy(order.at[:, :, pl.ds(g * SUB, SUB)], fields[g], load_sem.at[g])
        loads[g].start()
    solute_load = pltpu.make_async_copy(solute, held, solute_sem)
    solute_load.start()

    barrier = pltpu.get_barrier_semaphore()
    for peer in peers:
        pl.semaphore_signal(barrier, inc=1, device_id=(peer, tile), device_id_type=MESH)
    for d in range(GROUP):
        pl.semaphore_signal(barrier, inc=1, device_id=(lax.rem(v + d, GROUP), below), device_id_type=MESH)

    active_load.wait()
    blocks, weights = tile_blocks(active, tile)
    side_blocks = [tile_blocks(active, side)[0] for side in sides]

    sums = {}
    gathers, edges, row_copies = [], [], []

    def send_sums(g):
        loads[g].wait()
        for z in range(PLANES):
            total = jnp.zeros((SUB, COLS), F32)
            for k in range(KMAX):
                for i in range(BV):
                    one = fields[g][blocks[k] * BV + i, z]
                    total = total + one * one * weights[k]
            for p in range(GROUP):
                part[g, p, z] = total[:, p * LANES:(p + 1) * LANES]
        if g == PIECES[0]:
            pl.semaphore_wait(barrier, GROUP - 1 + GROUP)
        for d, peer in enumerate(peers):
            sums[g, d] = pltpu.make_async_remote_copy(
                part.at[g, peer], landed.at[g, d], sum_send.at[g, d], sum_recv.at[g, d],
                device_id=(peer, tile), device_id_type=MESH)
            sums[g, d].start()

    def send_rows(s):
        g, edge = (0, 0) if s == 0 else (GROUPS - 1, SUB - 1)
        for k in range(KMAX):
            block = side_blocks[s][k]
            weight = active[block, tile].astype(F32)
            for i in range(BV):
                slot = k * BV + i
                for z in range(PLANES):
                    row_out[s, z * SLOTS + slot:z * SLOTS + slot + 1, :] = (
                        fields[g][block * BV + i, z, edge:edge + 1, :] * weight)
        first = 0 if s == 0 else ROWS - 2
        for z in range(PLANES):
            row_out[s, 24 + 2 * z:26 + 2 * z, :] = held[z, first:first + 2, :]
        row_out[s, 30:32, :] = jnp.zeros((2, COLS), F32)
        copy = pltpu.make_async_remote_copy(
            row_out.at[s], row_in.at[1 - s], row_send.at[s], row_recv.at[1 - s],
            device_id=(v, sides[s]), device_id_type=MESH)
        copy.start()
        row_copies.append(copy)

    def local(k):
        for i in range(BV):
            slot = k * BV + i
            ones = [jnp.concatenate([field[blocks[k] * BV + i, z] for field in fields], axis=0)
                    for z in range(PLANES)]
            for z in range(PLANES):
                one = ones[z]
                shifted = held[z] - 0.05
                near = rows_sum(one) + cells_sum(one) + plane_sum(ones, z)
                value = one * (0.88 + 0.005 * (shifted * shifted) - 0.006 * (one * one)) + 0.02 * near
                base[slot, z] = value * weights[k]
                slope[slot, z] = one * (0.004 * weights[k])

    def reduce(g):
        total = part[g, v]
        for d in range(GROUP - 1):
            sums[g, d].wait_recv()
            total = total + landed[g, d]
        squares[g, v] = total
        for d, peer in enumerate(peers):
            copy = pltpu.make_async_remote_copy(
                squares.at[g, v], squares.at[g, v], all_send.at[g, d], all_recv.at[g, d],
                device_id=(peer, tile), device_id_type=MESH)
            copy.start()
            gathers.append(copy)
        if g in (0, GROUPS - 1):
            s, edge = (0, 0) if g == 0 else (1, SUB - 1)
            for z in range(PLANES):
                edge_out[s, z:z + 1, :] = total[z, edge:edge + 1, :]
            edge_out[s, 3:8, :] = jnp.zeros((5, LANES), F32)

    def send_edges(s):
        for d in range(GROUP):
            copy = pltpu.make_async_remote_copy(
                edge_out.at[s], edge_squares.at[1 - s, v], edge_send.at[s, d], edge_recv.at[1 - s, d],
                device_id=(lax.rem(v + d, GROUP), sides[s]), device_id_type=MESH)
            copy.start()
            edges.append(copy)

    for g in PIECES:
        send_sums(g)
    for d in range(GROUP):
        pl.semaphore_signal(near_sem, inc=1, device_id=(lax.rem(v + d, GROUP), above), device_id_type=MESH)
    solute_load.wait()
    send_rows(1)
    local(0)
    local(1)
    reduce(PIECES[0])
    local(2)
    reduce(PIECES[1])
    pl.semaphore_wait(near_sem, GROUP)
    send_edges(0)
    send_edges(1)
    send_rows(0)
    reduce(PIECES[2])
    local(3)
    reduce(PIECES[3])

    solutes = [held[z] for z in range(PLANES)]
    for z in range(PLANES):
        value = solutes[z]
        quiet[z] = bulk(value) + 6.0 * value - rows_sum(value) - cells_sum(value) - plane_sum(solutes, z)

    for copy in row_copies:
        copy.wait_recv()
    for s in range(2):
        row = 0 if s == 0 else ROWS - 1
        for k in range(KMAX):
            for i in range(BV):
                slot = k * BV + i
                for z in range(PLANES):
                    base[slot, z, row:row + 1, :] = base[slot, z, row:row + 1, :] + (
                        row_in[s, z * SLOTS + slot:z * SLOTS + slot + 1, :] * (0.02 * weights[k]))
        near_row, far_row = (1, 0) if s == 0 else (0, 1)
        nears = [row_in[s, 24 + 2 * z + near_row:25 + 2 * z + near_row, :] for z in range(PLANES)]
        for z in range(PLANES):
            far = row_in[s, 24 + 2 * z + far_row:25 + 2 * z + far_row, :]
            quiet[z, row:row + 1, :] = quiet[z, row:row + 1, :] - nears[z]
            around = far + held[z, row:row + 1, :] + cells_sum(nears[z]) + plane_sum(nears, z)
            edge_quiet[s, z:z + 1, :] = bulk(nears[z]) + 6.0 * nears[z] - around
            edge_held[s, z:z + 1, :] = nears[z]
        edge_quiet[s, 3:8, :] = jnp.zeros((5, COLS), F32)
        edge_held[s, 3:8, :] = jnp.zeros((5, COLS), F32)

    for copy in gathers + edges:
        copy.wait_recv()
    for copy in list(sums.values()) + gathers + edges + row_copies:
        copy.wait_send()


def finish(active_hbm, base, slope, squares, quiet, held, edge_quiet, edge_held, edge_squares, new_order, new_solute,
           active, active_sem, blank, stage, solute_stage, order_sem, solute_sem):
    tile = lax.axis_index("space")
    active_load = pltpu.make_async_copy(active_hbm, active, active_sem)
    active_load.start()
    blank[...] = jnp.zeros(blank.shape, F32)
    active_load.wait()
    flags = [active[b, tile] for b in range(BLOCKS)]
    for b in range(BLOCKS):
        @pl.when(flags[b] == 0)
        def _():
            pltpu.make_async_copy(blank, new_order.at[pl.ds(b * BV, BV)], order_sem.at[b]).start()
    totals = [
        jnp.concatenate(
            [jnp.concatenate([squares[g, p, z] for p in range(GROUP)], axis=1) for g in range(GROUPS)], axis=0)
        for z in range(PLANES)
    ]
    rank = jnp.int32(0)
    for b in range(BLOCKS):
        @pl.when(flags[b] != 0)
        def _(rank=rank):
            for i in range(BV):
                for z in range(PLANES):
                    stage[rank, i, z] = base[rank * BV + i, z] - slope[rank * BV + i, z] * totals[z]
            pltpu.make_async_copy(stage.at[rank], new_order.at[pl.ds(b * BV, BV)], order_sem.at[b]).start()
        rank = rank + flags[b]

    pots = []
    for z in range(PLANES):
        pots.append(quiet[z] - 0.5 * (held[z] - 0.05) * totals[z])
    ends = []
    for s in range(2):
        total = jnp.concatenate([edge_squares[s, p] for p in range(GROUP)], axis=1)
        ends.append(edge_quiet[s] - 0.5 * (edge_held[s] - 0.05) * total)
    row = lax.broadcasted_iota(jnp.int32, (ROWS, COLS), 0)
    for z in range(PLANES):
        value = pots[z]
        before = jnp.where(row == 0, jnp.broadcast_to(ends[0][z:z + 1, :], (ROWS, COLS)), pltpu.roll(value, 1, 0))
        after = jnp.where(row == ROWS - 1, jnp.broadcast_to(ends[1][z:z + 1, :], (ROWS, COLS)),
                          pltpu.roll(value, ROWS - 1, 0))
        lap = before + after + cells_sum(value) + plane_sum(pots, z) - 6.0 * value
        solute_stage[z] = held[z] + 0.01 * lap
    out = pltpu.make_async_copy(solute_stage, new_solute, solute_sem)
    out.start()
    for b in range(BLOCKS):
        pltpu.make_async_copy(blank, new_order.at[pl.ds(b * BV, BV)], order_sem.at[b]).wait()
    out.wait()


def shards(order, solute, active):
    vmem = pl.BlockSpec(memory_space=pltpu.VMEM)
    hbm = pl.BlockSpec(memory_space=pltpu.HBM)
    dma = pltpu.SemaphoreType.DMA
    handed = [
        (SLOTS, PLANES, ROWS, COLS),
        (SLOTS, PLANES, ROWS, COLS),
        (GROUPS, GROUP, PLANES, SUB, LANES),
        (PLANES, ROWS, COLS),
        (PLANES, ROWS, COLS),
        (2, 8, COLS),
        (2, 8, COLS),
        (2, GROUP, 8, LANES),
    ]
    order, solute, flags = (
        pltpu.with_memory_space_constraint(value, pltpu.HBM) for value in (order, solute, active.T))
    results = pl.pallas_call(
        exchange,
        out_shape=[pltpu.VMEM(shape, F32) for shape in handed],
        in_specs=[hbm, hbm, hbm],
        out_specs=[vmem] * len(handed),
        scratch_shapes=[
            pltpu.VMEM((VARIANTS, PLANES, SUB, COLS), F32),
            pltpu.VMEM((VARIANTS, PLANES, SUB, COLS), F32),
            pltpu.VMEM((VARIANTS, PLANES, SUB, COLS), F32),
            pltpu.VMEM((VARIANTS, PLANES, SUB, COLS), F32),
            pltpu.VMEM((GROUPS, GROUP, PLANES, SUB, LANES), F32),
            pltpu.VMEM((GROUPS, GROUP - 1, PLANES, SUB, LANES), F32),
            pltpu.VMEM((2, 32, COLS), F32),
            pltpu.VMEM((2, 32, COLS), F32),
            pltpu.VMEM((2, 8, LANES), F32),
            pltpu.SMEM((BLOCKS, TILES), jnp.int32),
            dma,
            dma((GROUPS,)),
            dma,
            pltpu.SemaphoreType.REGULAR,
            dma((2,)),
            dma((2,)),
            dma((GROUPS, GROUP - 1)),
            dma((GROUPS, GROUP - 1)),
            dma((GROUPS, GROUP - 1)),
            dma((GROUPS, GROUP - 1)),
            dma((2, GROUP)),
            dma((2, GROUP)),
        ],
        compiler_params=pltpu.CompilerParams(
            collective_id=0, has_side_effects=True, vmem_limit_bytes=32 << 20),
        name="exchange",
    )(order, solute, flags)
    return pl.pallas_call(
        finish,
        out_shape=[
            jax.ShapeDtypeStruct(order.shape, F32),
            jax.ShapeDtypeStruct(solute.shape, F32),
        ],
        in_specs=[hbm] + [vmem] * len(handed),
        out_specs=[hbm, hbm],
        scratch_shapes=[
            pltpu.SMEM((BLOCKS, TILES), jnp.int32),
            dma,
            pltpu.VMEM((BV, PLANES, ROWS, COLS), F32),
            pltpu.VMEM((KMAX, BV, PLANES, ROWS, COLS), F32),
            pltpu.VMEM((PLANES, ROWS, COLS), F32),
            dma((BLOCKS,)),
            dma,
        ],
        compiler_params=pltpu.CompilerParams(vmem_limit_bytes=32 << 20),
        name="finish",
    )(flags, *results)


def solution(mesh):
    return jax.shard_map(
        shards,
        mesh=mesh,
        in_specs=(P("var", None, "space", None), P(None, "space", None), P(None, "var")),
        out_specs=(P("var", None, "space", None), P(None, "space", None)),
        check_vma=False,
    )
```

```python
import functools

import jax
import jax.numpy as jnp
from jax import lax
from jax.experimental import pallas as pl
from jax.experimental.pallas import tpu as pltpu
from jax.sharding import PartitionSpec as P

MESH = pl.DeviceIdType.MESH
F32 = jnp.float32
PLANES, ROWS, COLS, LANES = 3, 32, 1024, 128
VARIANTS, BLOCKS, BV, KMAX = 16, 8, 2, 4
SLOTS = KMAX * BV
GROUP, TILES = 8, 32
HALF = TILES // 2
SUB, GROUPS = 8, 4
PIECES = (3, 0, 1, 2)
ROUTES = ("x", "direct", "direct", "y")
PEERS = ((1, 0), (0, 1), (3, 0), (2, 1), (1, 1), (2, 0), (3, 1))


def tile_blocks(active_ref, tile):
    flags = [active_ref[b, tile] for b in range(BLOCKS)]
    blocks = [jnp.int32(0)] * KMAX
    rank = jnp.int32(0)
    for b in range(BLOCKS):
        for k in range(KMAX):
            hit = jnp.where(rank == k, flags[b], 0)
            blocks[k] = blocks[k] + b * hit
        rank = rank + flags[b]
    weights = [jnp.where(rank > k, 1.0, 0.0).astype(F32) for k in range(KMAX)]
    return blocks, weights


def rows_sum(value):
    row = lax.broadcasted_iota(jnp.int32, value.shape, 0)
    before = jnp.where(row == 0, 0.0, pltpu.roll(value, 1, 0))
    after = jnp.where(row == value.shape[0] - 1, 0.0, pltpu.roll(value, value.shape[0] - 1, 0))
    return before + after


def cells_sum(value):
    return pltpu.roll(value, 1, 1) + pltpu.roll(value, value.shape[1] - 1, 1)


def plane_sum(planes, z):
    return planes[min(z + 1, PLANES - 1)] + planes[max(z - 1, 0)]


def bulk(value):
    middle = value - 0.5
    shifted = value - 0.05
    gap = value - 0.95
    return (-2.0 * middle + 9.88 * middle * middle * middle
            + 2.0 * shifted * shifted * shifted + 2.0 * gap * gap * gap)


def exchange(order, solute, active_hbm, base, slope, squares, quiet, held, edge_quiet, edge_held, edge_squares,
             field0, field1, field2, field3, part, landed, row_out, row_in, edge_out,
             picked, scale, active, active_sem, load_sem, solute_sem, near_sem, row_send, row_recv,
             sum_send, sum_recv, all_send, all_recv, edge_send, edge_recv):
    v, tile = lax.axis_index("var"), lax.axis_index("space")
    x, y = v // 2, v % 2
    below, above = lax.rem(tile + TILES - 1, TILES), lax.rem(tile + 1, TILES)
    sides = (below, above)
    peers = [lax.rem(x + dx, 4) * 2 + (y + dy - 2 * y * dy) for dx, dy in PEERS]
    fields = (field0, field1, field2, field3)

    active_load = pltpu.make_async_copy(active_hbm, active, active_sem)
    active_load.start()
    loads = {}
    for g in PIECES:
        loads[g] = pltpu.make_async_copy(order.at[:, :, pl.ds(g * SUB, SUB)], fields[g], load_sem.at[g])
        loads[g].start()
    solute_load = pltpu.make_async_copy(solute, held, solute_sem)
    solute_load.start()

    first = jnp.where(lax.rem(tile, HALF) == 0, 1, 0)
    last = jnp.where(lax.rem(tile, HALF) == HALF - 1, 1, 0)

    def report(semaphore, side):
        for d in range(GROUP):
            pl.semaphore_signal(semaphore, inc=1, device_id=(lax.rem(v + d, GROUP), side), device_id_type=MESH)

    barrier = pltpu.get_barrier_semaphore()
    for peer in peers:
        pl.semaphore_signal(barrier, inc=1, device_id=(peer, tile), device_id_type=MESH)
    pl.when(last == 0)(lambda: report(barrier, above))
    pl.when(first == 1)(lambda: report(barrier, below))

    active_load.wait()
    blocks, weights = tile_blocks(active, tile)
    for k in range(KMAX):
        picked[k] = blocks[k]
        scale[k] = weights[k]
    side_blocks = [tile_blocks(active, side)[0] for side in sides]

    sums = {}
    gathers, arrived, row_copies = {}, set(), []

    def send_sums(g):
        loads[g].wait()
        for z in range(PLANES):
            total = jnp.zeros((SUB, COLS), F32)
            for k in range(KMAX):
                for i in range(BV):
                    one = fields[g][blocks[k] * BV + i, z]
                    total = total + one * one * weights[k]
            for p in range(GROUP):
                part[g, p, z] = total[:, p * LANES:(p + 1) * LANES]
        if g == PIECES[0]:
            pl.semaphore_wait(barrier, GROUP - 1 + GROUP * (1 - first + last))
        for d, peer in enumerate(peers):
            sums[g, d] = pltpu.make_async_remote_copy(
                part.at[g, peer], landed.at[g, d], sum_send.at[g, d], sum_recv.at[g, d],
                device_id=(peer, tile), device_id_type=MESH)
            sums[g, d].start()

    def stage_rows(s):
        g, edge = (0, 0) if s == 0 else (GROUPS - 1, SUB - 1)
        for k in range(KMAX):
            block = side_blocks[s][k]
            weight = active[block, tile].astype(F32)
            for i in range(BV):
                slot = k * BV + i
                for z in range(PLANES):
                    row_out[s, z * SLOTS + slot:z * SLOTS + slot + 1, :] = (
                        fields[g][block * BV + i, z, edge:edge + 1, :] * weight)
        first = 0 if s == 0 else ROWS - 2
        for z in range(PLANES):
            row_out[s, 24 + 2 * z:26 + 2 * z, :] = held[z, first:first + 2, :]
        row_out[s, 30:32, :] = jnp.zeros((2, COLS), F32)
        row_copies.append(pltpu.make_async_remote_copy(
            row_out.at[s], row_in.at[1 - s], row_send.at[s], row_recv.at[1 - s],
            device_id=(v, sides[s]), device_id_type=MESH))

    def local(k, carry):
        for i in range(BV):
            slot = k * BV + i
            weight = scale[k]
            ones = [jnp.concatenate([field[picked[k] * BV + i, z] for field in fields], axis=0)
                    for z in range(PLANES)]
            for z in range(PLANES):
                one = ones[z]
                shifted = held[z] - 0.05
                near = rows_sum(one) + cells_sum(one) + plane_sum(ones, z)
                value = one * (0.88 + 0.005 * (shifted * shifted) - 0.006 * (one * one)) + 0.02 * near
                base[slot, z] = value * weight
                slope[slot, z] = one * (0.004 * weight)
        return carry

    def gather(g, d, chunk, peer):
        gathers[g, d] = pltpu.make_async_remote_copy(
            squares.at[g, chunk], squares.at[g, chunk], all_send.at[g, d], all_recv.at[g, d],
            device_id=(peer, tile), device_id_type=MESH)
        gathers[g, d].start()

    def arrive(g, d):
        gathers[g, d].wait_recv()
        arrived.add((g, d))

    def forward(g):
        flip = PEERS.index((0, 1))
        if ROUTES[g] == "y":
            arrive(g, flip)
        for dx in (2, 1, 3):
            if ROUTES[g] == "y":
                gather(g, PEERS.index((dx, 1)), peers[flip], peers[PEERS.index((dx, 0))])
            elif ROUTES[g] == "x":
                arrive(g, PEERS.index((dx, 0)))
                gather(g, PEERS.index((dx, 1)), lax.rem(x + 4 - dx, 4) * 2 + y, peers[flip])

    def reduce(g):
        total = part[g, v]
        for d in range(GROUP - 1):
            sums[g, d].wait_recv()
            total = total + landed[g, d]
        squares[g, v] = total
        for d, (dx, dy) in enumerate(PEERS):
            if ROUTES[g] == "direct" or dx == 0 or dy == 0:
                gather(g, d, v, peers[d])
        if g in (0, GROUPS - 1):
            s, edge = (0, 0) if g == 0 else (1, SUB - 1)
            for z in range(PLANES):
                edge_out[s, z:z + 1, :] = total[z, edge:edge + 1, :]

    def start(copies):
        for copy in copies:
            copy.start()

    edges = [
        [pltpu.make_async_remote_copy(
            edge_out.at[s, 0:PLANES], edge_squares.at[1 - s, v, 0:PLANES], edge_send.at[s, d], edge_recv.at[1 - s, d],
            device_id=(lax.rem(v + d, GROUP), sides[s]), device_id_type=MESH) for d in range(GROUP)]
        for s in range(2)
    ]

    for g in PIECES:
        send_sums(g)
        if g == PIECES[0]:
            pl.when(first == 0)(lambda: report(near_sem.at[1], below))
            pl.when(last == 1)(lambda: report(near_sem.at[0], above))
    solute_load.wait()
    stage_rows(0)
    stage_rows(1)

    pl.when(last == 0)(lambda: pl.semaphore_wait(near_sem.at[1], GROUP))
    row_copies[1].start()
    pl.when(first == 0)(lambda: row_copies[0].start())
    lax.fori_loop(0, 1, local, 0)
    reduce(PIECES[0])
    start(edges[1])
    reduce(PIECES[1])
    pl.when(first == 0)(lambda: start(edges[0]))
    reduce(PIECES[2])
    forward(PIECES[0])
    reduce(PIECES[3])
    forward(PIECES[1])

    @pl.when(first == 1)
    def _():
        pl.semaphore_wait(near_sem.at[0], GROUP)
        start(edges[0])
        row_copies[0].start()

    lax.fori_loop(1, 2, local, 0)
    forward(PIECES[2])
    lax.fori_loop(2, 4, local, 0)

    solutes = [held[z] for z in range(PLANES)]
    for z in range(PLANES):
        value = solutes[z]
        quiet[z] = bulk(value) + 6.0 * value - rows_sum(value) - cells_sum(value) - plane_sum(solutes, z)

    for copy in row_copies:
        copy.wait_recv()
    for s in range(2):
        row = 0 if s == 0 else ROWS - 1
        for k in range(KMAX):
            for i in range(BV):
                slot = k * BV + i
                for z in range(PLANES):
                    base[slot, z, row:row + 1, :] = base[slot, z, row:row + 1, :] + (
                        row_in[s, z * SLOTS + slot:z * SLOTS + slot + 1, :] * (0.02 * weights[k]))
        near_row, far_row = (1, 0) if s == 0 else (0, 1)
        nears = [row_in[s, 24 + 2 * z + near_row:25 + 2 * z + near_row, :] for z in range(PLANES)]
        for z in range(PLANES):
            far = row_in[s, 24 + 2 * z + far_row:25 + 2 * z + far_row, :]
            quiet[z, row:row + 1, :] = quiet[z, row:row + 1, :] - nears[z]
            around = far + held[z, row:row + 1, :] + cells_sum(nears[z]) + plane_sum(nears, z)
            edge_quiet[s, z:z + 1, :] = bulk(nears[z]) + 6.0 * nears[z] - around
            edge_held[s, z:z + 1, :] = nears[z]

    edges = edges[0] + edges[1]
    for place in gathers:
        if place not in arrived:
            gathers[place].wait_recv()
    for copy in edges:
        copy.wait_recv()
    for copy in list(sums.values()) + list(gathers.values()) + edges + row_copies:
        copy.wait_send()


def finish(active_hbm, base, slope, squares, quiet, held, edge_quiet, edge_held, edge_squares, new_order, new_solute,
           active, active_sem, blank, stage, solute_stage, order_sem, solute_sem):
    tile = lax.axis_index("space")
    active_load = pltpu.make_async_copy(active_hbm, active, active_sem)
    active_load.start()
    blank[...] = jnp.zeros(blank.shape, F32)
    active_load.wait()

    def clear(b, carry):
        @pl.when(active[b, tile] == 0)
        def _():
            pltpu.make_async_copy(blank, new_order.at[pl.ds(b * BV, BV)], order_sem.at[b]).start()
        return carry

    lax.fori_loop(0, BLOCKS, clear, 0)
    totals = [
        jnp.concatenate(
            [jnp.concatenate([squares[g, p, z] for p in range(GROUP)], axis=1) for g in range(GROUPS)], axis=0)
        for z in range(PLANES)
    ]

    def update(b, rank):
        flag = active[b, tile]

        @pl.when(flag != 0)
        def _():
            for i in range(BV):
                for z in range(PLANES):
                    stage[rank, i, z] = base[rank * BV + i, z] - slope[rank * BV + i, z] * totals[z]
            pltpu.make_async_copy(stage.at[rank], new_order.at[pl.ds(b * BV, BV)], order_sem.at[b]).start()
        return rank + flag

    lax.fori_loop(0, BLOCKS, update, jnp.int32(0))
    pots = []
    for z in range(PLANES):
        pots.append(quiet[z] - 0.5 * (held[z] - 0.05) * totals[z])
    ends = []
    for s in range(2):
        total = jnp.concatenate([edge_squares[s, p, 0:PLANES] for p in range(GROUP)], axis=1)
        ends.append(edge_quiet[s, 0:PLANES] - 0.5 * (edge_held[s, 0:PLANES] - 0.05) * total)
    row = lax.broadcasted_iota(jnp.int32, (ROWS, COLS), 0)
    for z in range(PLANES):
        value = pots[z]
        before = jnp.where(row == 0, jnp.broadcast_to(ends[0][z:z + 1, :], (ROWS, COLS)), pltpu.roll(value, 1, 0))
        after = jnp.where(row == ROWS - 1, jnp.broadcast_to(ends[1][z:z + 1, :], (ROWS, COLS)),
                          pltpu.roll(value, ROWS - 1, 0))
        lap = before + after + cells_sum(value) + plane_sum(pots, z) - 6.0 * value
        solute_stage[z] = held[z] + 0.01 * lap
    out = pltpu.make_async_copy(solute_stage, new_solute, solute_sem)
    out.start()
    for b in range(BLOCKS):
        pltpu.make_async_copy(blank, new_order.at[pl.ds(b * BV, BV)], order_sem.at[b]).wait()
    out.wait()


def shards(order, solute, active):
    vmem = pl.BlockSpec(memory_space=pltpu.VMEM)
    hbm = pl.BlockSpec(memory_space=pltpu.HBM)
    dma = pltpu.SemaphoreType.DMA
    handed = [
        (SLOTS, PLANES, ROWS, COLS),
        (SLOTS, PLANES, ROWS, COLS),
        (GROUPS, GROUP, PLANES, SUB, LANES),
        (PLANES, ROWS, COLS),
        (PLANES, ROWS, COLS),
        (2, 8, COLS),
        (2, 8, COLS),
        (2, GROUP, 8, LANES),
    ]
    order, solute, flags = (
        pltpu.with_memory_space_constraint(value, pltpu.HBM) for value in (order, solute, active.T))
    results = pl.pallas_call(
        exchange,
        out_shape=[pltpu.VMEM(shape, F32) for shape in handed],
        in_specs=[hbm, hbm, hbm],
        out_specs=[vmem] * len(handed),
        scratch_shapes=[
            pltpu.VMEM((VARIANTS, PLANES, SUB, COLS), F32),
            pltpu.VMEM((VARIANTS, PLANES, SUB, COLS), F32),
            pltpu.VMEM((VARIANTS, PLANES, SUB, COLS), F32),
            pltpu.VMEM((VARIANTS, PLANES, SUB, COLS), F32),
            pltpu.VMEM((GROUPS, GROUP, PLANES, SUB, LANES), F32),
            pltpu.VMEM((GROUPS, GROUP - 1, PLANES, SUB, LANES), F32),
            pltpu.VMEM((2, 32, COLS), F32),
            pltpu.VMEM((2, 32, COLS), F32),
            pltpu.VMEM((2, 8, LANES), F32),
            pltpu.SMEM((KMAX,), jnp.int32),
            pltpu.SMEM((KMAX,), F32),
            pltpu.SMEM((BLOCKS, TILES), jnp.int32),
            dma,
            dma((GROUPS,)),
            dma,
            pltpu.SemaphoreType.REGULAR((2,)),
            dma((2,)),
            dma((2,)),
            dma((GROUPS, GROUP - 1)),
            dma((GROUPS, GROUP - 1)),
            dma((GROUPS, GROUP - 1)),
            dma((GROUPS, GROUP - 1)),
            dma((2, GROUP)),
            dma((2, GROUP)),
        ],
        compiler_params=pltpu.CompilerParams(
            collective_id=0, has_side_effects=True, vmem_limit_bytes=32 << 20),
        name="exchange",
    )(order, solute, flags)
    return pl.pallas_call(
        finish,
        out_shape=[
            jax.ShapeDtypeStruct(order.shape, F32),
            jax.ShapeDtypeStruct(solute.shape, F32),
        ],
        in_specs=[hbm] + [vmem] * len(handed),
        out_specs=[hbm, hbm],
        scratch_shapes=[
            pltpu.SMEM((BLOCKS, TILES), jnp.int32),
            dma,
            pltpu.VMEM((BV, PLANES, ROWS, COLS), F32),
            pltpu.VMEM((KMAX, BV, PLANES, ROWS, COLS), F32),
            pltpu.VMEM((PLANES, ROWS, COLS), F32),
            dma((BLOCKS,)),
            dma,
        ],
        compiler_params=pltpu.CompilerParams(vmem_limit_bytes=32 << 20),
        name="finish",
    )(flags, *results)


def solution(mesh):
    return jax.shard_map(
        shards,
        mesh=mesh,
        in_specs=(P("var", None, "space", None), P(None, "space", None), P(None, "var")),
        out_specs=(P("var", None, "space", None), P(None, "space", None)),
        check_vma=False,
    )
```

```python
import functools

import jax
import jax.numpy as jnp
from jax import lax
from jax.experimental import pallas as pl
from jax.experimental.pallas import tpu as pltpu
from jax.sharding import PartitionSpec as P

MESH = pl.DeviceIdType.MESH
F32 = jnp.float32
PLANES, ROWS, COLS, LANES = 3, 32, 1024, 128
VARIANTS, BLOCKS, BV, KMAX = 16, 8, 2, 4
SLOTS = KMAX * BV
GROUP, TILES = 8, 32
HALF = TILES // 2
SUB, GROUPS = 8, 4
PIECES = (3, 0, 1, 2)
ROUTES = ("x", "direct", "direct", "y")
PEERS = ((2, 1), (1, 1), (3, 1), (2, 0), (0, 1), (1, 0), (3, 0))


def tile_blocks(active_ref, tile):
    flags = [active_ref[b, tile] for b in range(BLOCKS)]
    blocks = [jnp.int32(0)] * KMAX
    rank = jnp.int32(0)
    for b in range(BLOCKS):
        for k in range(KMAX):
            hit = jnp.where(rank == k, flags[b], 0)
            blocks[k] = blocks[k] + b * hit
        rank = rank + flags[b]
    weights = [jnp.where(rank > k, 1.0, 0.0).astype(F32) for k in range(KMAX)]
    return blocks, weights


def rows_sum(value):
    row = lax.broadcasted_iota(jnp.int32, value.shape, 0)
    before = jnp.where(row == 0, 0.0, pltpu.roll(value, 1, 0))
    after = jnp.where(row == value.shape[0] - 1, 0.0, pltpu.roll(value, value.shape[0] - 1, 0))
    return before + after


def cells_sum(value):
    return pltpu.roll(value, 1, 1) + pltpu.roll(value, value.shape[1] - 1, 1)


def plane_sum(planes, z):
    return planes[min(z + 1, PLANES - 1)] + planes[max(z - 1, 0)]


def bulk(value):
    middle = value - 0.5
    shifted = value - 0.05
    gap = value - 0.95
    return (-2.0 * middle + 9.88 * middle * middle * middle
            + 2.0 * shifted * shifted * shifted + 2.0 * gap * gap * gap)


def exchange(order, solute, active_hbm, base, slope, squares, quiet, held, edge_quiet, edge_held, edge_squares,
             blank, code,
             field0, field1, field2, field3, part, landed, row_out, row_in, edge_out,
             picked, scale, active, active_sem, load_sem, solute_sem, near_sem, row_send, row_recv,
             sum_send, sum_recv, all_send, all_recv, edge_send, edge_recv):
    v, tile = lax.axis_index("var"), lax.axis_index("space")
    x, y = v // 2, v % 2
    below, above = lax.rem(tile + TILES - 1, TILES), lax.rem(tile + 1, TILES)
    sides = (below, above)
    peers = [lax.rem(x + dx, 4) * 2 + (y + dy - 2 * y * dy) for dx, dy in PEERS]
    fields = (field0, field1, field2, field3)

    active_load = pltpu.make_async_copy(active_hbm, active, active_sem)
    active_load.start()
    loads = {}
    for g in PIECES:
        loads[g] = pltpu.make_async_copy(order.at[:, :, pl.ds(g * SUB, SUB)], fields[g], load_sem.at[g])
        loads[g].start()
    solute_load = pltpu.make_async_copy(solute, held, solute_sem)
    solute_load.start()

    first = jnp.where(lax.rem(tile, HALF) == 0, 1, 0)
    last = jnp.where(lax.rem(tile, HALF) == HALF - 1, 1, 0)

    def report(semaphore, side):
        for d in range(GROUP):
            pl.semaphore_signal(semaphore, inc=1, device_id=(lax.rem(v + d, GROUP), side), device_id_type=MESH)

    barrier = pltpu.get_barrier_semaphore()
    for peer in peers:
        pl.semaphore_signal(barrier, inc=1, device_id=(peer, tile), device_id_type=MESH)
    pl.when(last == 0)(lambda: report(barrier, above))
    pl.when(first == 1)(lambda: report(barrier, below))

    active_load.wait()
    blocks, weights = tile_blocks(active, tile)
    for k in range(KMAX):
        picked[k] = blocks[k]
        scale[k] = weights[k]
    side_blocks = [tile_blocks(active, side)[0] for side in sides]

    sums = {}
    gathers, arrived, row_copies = {}, set(), []

    def send_sums(g):
        loads[g].wait()
        for z in range(PLANES):
            total = jnp.zeros((SUB, COLS), F32)
            for k in range(KMAX):
                for i in range(BV):
                    one = fields[g][blocks[k] * BV + i, z]
                    total = total + one * one * weights[k]
            for p in range(GROUP):
                part[g, p, z] = total[:, p * LANES:(p + 1) * LANES]
        if g == PIECES[0]:
            pl.semaphore_wait(barrier, GROUP - 1 + GROUP * (1 - first + last))
        for d, peer in enumerate(peers):
            sums[g, d] = pltpu.make_async_remote_copy(
                part.at[g, peer], landed.at[g, d], sum_send.at[g, d], sum_recv.at[g, d],
                device_id=(peer, tile), device_id_type=MESH)
            sums[g, d].start()

    def stage_rows(s):
        g, edge = (0, 0) if s == 0 else (GROUPS - 1, SUB - 1)
        for k in range(KMAX):
            block = side_blocks[s][k]
            weight = active[block, tile].astype(F32)
            for i in range(BV):
                slot = k * BV + i
                for z in range(PLANES):
                    row_out[s, z * SLOTS + slot:z * SLOTS + slot + 1, :] = (
                        fields[g][block * BV + i, z, edge:edge + 1, :] * weight)
        first = 0 if s == 0 else ROWS - 2
        for z in range(PLANES):
            row_out[s, 24 + 2 * z:26 + 2 * z, :] = held[z, first:first + 2, :]
        row_out[s, 30:32, :] = jnp.zeros((2, COLS), F32)
        row_copies.append(pltpu.make_async_remote_copy(
            row_out.at[s], row_in.at[1 - s], row_send.at[s], row_recv.at[1 - s],
            device_id=(v, sides[s]), device_id_type=MESH))

    def local(k, carry):
        for i in range(BV):
            slot = k * BV + i
            weight = scale[k]
            ones = [jnp.concatenate([field[picked[k] * BV + i, z] for field in fields], axis=0)
                    for z in range(PLANES)]
            for z in range(PLANES):
                one = ones[z]
                shifted = held[z] - 0.05
                near = rows_sum(one) + cells_sum(one) + plane_sum(ones, z)
                value = one * (0.88 + 0.005 * (shifted * shifted) - 0.006 * (one * one)) + 0.02 * near
                base[slot, z] = value * weight
                slope[slot, z] = one * (0.004 * weight)
        return carry

    def gather(g, d, chunk, peer):
        gathers[g, d] = pltpu.make_async_remote_copy(
            squares.at[g, chunk], squares.at[g, chunk], all_send.at[g, d], all_recv.at[g, d],
            device_id=(peer, tile), device_id_type=MESH)
        gathers[g, d].start()

    def arrive(g, d):
        gathers[g, d].wait_recv()
        arrived.add((g, d))

    def forward(g):
        flip = PEERS.index((0, 1))
        if ROUTES[g] == "y":
            arrive(g, flip)
        for dx in (2, 1, 3):
            if ROUTES[g] == "y":
                gather(g, PEERS.index((dx, 1)), peers[flip], peers[PEERS.index((dx, 0))])
            elif ROUTES[g] == "x":
                arrive(g, PEERS.index((dx, 0)))
                gather(g, PEERS.index((dx, 1)), lax.rem(x + 4 - dx, 4) * 2 + y, peers[flip])

    def reduce(g):
        total = part[g, v]
        for d in range(GROUP - 1):
            sums[g, d].wait_recv()
            total = total + landed[g, d]
        squares[g, v] = total
        for d, (dx, dy) in enumerate(PEERS):
            if ROUTES[g] == "direct" or dx == 0 or dy == 0:
                gather(g, d, v, peers[d])
        if g in (0, GROUPS - 1):
            s, edge = (0, 0) if g == 0 else (1, SUB - 1)
            for z in range(PLANES):
                edge_out[s, z:z + 1, :] = total[z, edge:edge + 1, :]

    def start(copies):
        for copy in copies:
            copy.start()

    edges = [
        [pltpu.make_async_remote_copy(
            edge_out.at[s, 0:PLANES], edge_squares.at[1 - s, v, 0:PLANES], edge_send.at[s, d], edge_recv.at[1 - s, d],
            device_id=(lax.rem(v + d, GROUP), sides[s]), device_id_type=MESH) for d in range(GROUP)]
        for s in range(2)
    ]

    for g in PIECES:
        send_sums(g)
        if g == PIECES[0]:
            pl.when(first == 0)(lambda: report(near_sem.at[1], below))
            pl.when(last == 1)(lambda: report(near_sem.at[0], above))
    solute_load.wait()
    stage_rows(0)
    stage_rows(1)

    pl.when(last == 0)(lambda: pl.semaphore_wait(near_sem.at[1], GROUP))
    row_copies[1].start()
    pl.when(first == 0)(lambda: row_copies[0].start())
    blank[...] = jnp.zeros(blank.shape, F32)
    bits = jnp.int32(0)
    for b in range(BLOCKS):
        bits = bits + active[b, tile] * (1 << b)
    code[...] = jnp.full(code.shape, bits.astype(F32), F32)
    lax.fori_loop(0, 1, local, 0)
    reduce(PIECES[0])
    start(edges[1])
    reduce(PIECES[1])
    pl.when(first == 0)(lambda: start(edges[0]))
    reduce(PIECES[2])
    forward(PIECES[0])
    reduce(PIECES[3])
    forward(PIECES[1])

    @pl.when(first == 1)
    def _():
        pl.semaphore_wait(near_sem.at[0], GROUP)
        start(edges[0])
        row_copies[0].start()

    lax.fori_loop(1, 2, local, 0)
    forward(PIECES[2])
    lax.fori_loop(2, 4, local, 0)

    solutes = [held[z] for z in range(PLANES)]
    for z in range(PLANES):
        value = solutes[z]
        quiet[z] = bulk(value) + 6.0 * value - rows_sum(value) - cells_sum(value) - plane_sum(solutes, z)

    for copy in row_copies:
        copy.wait_recv()
    for s in range(2):
        row = 0 if s == 0 else ROWS - 1
        for k in range(KMAX):
            for i in range(BV):
                slot = k * BV + i
                for z in range(PLANES):
                    base[slot, z, row:row + 1, :] = base[slot, z, row:row + 1, :] + (
                        row_in[s, z * SLOTS + slot:z * SLOTS + slot + 1, :] * (0.02 * weights[k]))
        near_row, far_row = (1, 0) if s == 0 else (0, 1)
        nears = [row_in[s, 24 + 2 * z + near_row:25 + 2 * z + near_row, :] for z in range(PLANES)]
        for z in range(PLANES):
            far = row_in[s, 24 + 2 * z + far_row:25 + 2 * z + far_row, :]
            quiet[z, row:row + 1, :] = quiet[z, row:row + 1, :] - nears[z]
            around = far + held[z, row:row + 1, :] + cells_sum(nears[z]) + plane_sum(nears, z)
            edge_quiet[s, z:z + 1, :] = bulk(nears[z]) + 6.0 * nears[z] - around
            edge_held[s, z:z + 1, :] = nears[z]

    edges = edges[0] + edges[1]
    for place in gathers:
        if place not in arrived:
            gathers[place].wait_recv()
    for copy in edges:
        copy.wait_recv()
    for copy in list(sums.values()) + list(gathers.values()) + edges + row_copies:
        copy.wait_send()


def finish(base, slope, squares, quiet, held, edge_quiet, edge_held, edge_squares, blank, code, new_order, new_solute,
           stage, solute_stage, order_sem, solute_sem):
    bits = jnp.max(code[...]).astype(jnp.int32)

    def flag_of(b):
        return lax.bitwise_and(lax.shift_right_logical(bits, b), 1)

    def clear(b, carry):
        @pl.when(flag_of(b) == 0)
        def _():
            pltpu.make_async_copy(blank, new_order.at[pl.ds(b * BV, BV)], order_sem.at[b]).start()
        return carry

    lax.fori_loop(0, BLOCKS, clear, 0)
    totals = [
        jnp.concatenate(
            [jnp.concatenate([squares[g, p, z] for p in range(GROUP)], axis=1) for g in range(GROUPS)], axis=0)
        for z in range(PLANES)
    ]

    def update(b, rank):
        flag = flag_of(b)

        @pl.when(flag != 0)
        def _():
            for i in range(BV):
                for z in range(PLANES):
                    stage[rank, i, z] = base[rank * BV + i, z] - slope[rank * BV + i, z] * totals[z]
            pltpu.make_async_copy(stage.at[rank], new_order.at[pl.ds(b * BV, BV)], order_sem.at[b]).start()
        return rank + flag

    lax.fori_loop(0, BLOCKS, update, jnp.int32(0))
    pots = []
    for z in range(PLANES):
        pots.append(quiet[z] - 0.5 * (held[z] - 0.05) * totals[z])
    ends = []
    for s in range(2):
        total = jnp.concatenate([edge_squares[s, p, 0:PLANES] for p in range(GROUP)], axis=1)
        ends.append(edge_quiet[s, 0:PLANES] - 0.5 * (edge_held[s, 0:PLANES] - 0.05) * total)
    row = lax.broadcasted_iota(jnp.int32, (ROWS, COLS), 0)
    for z in range(PLANES):
        value = pots[z]
        before = jnp.where(row == 0, jnp.broadcast_to(ends[0][z:z + 1, :], (ROWS, COLS)), pltpu.roll(value, 1, 0))
        after = jnp.where(row == ROWS - 1, jnp.broadcast_to(ends[1][z:z + 1, :], (ROWS, COLS)),
                          pltpu.roll(value, ROWS - 1, 0))
        lap = before + after + cells_sum(value) + plane_sum(pots, z) - 6.0 * value
        solute_stage[z] = held[z] + 0.01 * lap
    out = pltpu.make_async_copy(solute_stage, new_solute, solute_sem)
    out.start()
    for b in range(BLOCKS):
        pltpu.make_async_copy(blank, new_order.at[pl.ds(b * BV, BV)], order_sem.at[b]).wait()
    out.wait()


def shards(order, solute, active):
    vmem = pl.BlockSpec(memory_space=pltpu.VMEM)
    hbm = pl.BlockSpec(memory_space=pltpu.HBM)
    dma = pltpu.SemaphoreType.DMA
    handed = [
        (SLOTS, PLANES, ROWS, COLS),
        (SLOTS, PLANES, ROWS, COLS),
        (GROUPS, GROUP, PLANES, SUB, LANES),
        (PLANES, ROWS, COLS),
        (PLANES, ROWS, COLS),
        (2, 8, COLS),
        (2, 8, COLS),
        (2, GROUP, 8, LANES),
        (BV, PLANES, ROWS, COLS),
        (8, LANES),
    ]
    order, solute, flags = (
        pltpu.with_memory_space_constraint(value, pltpu.HBM) for value in (order, solute, active.T))
    results = pl.pallas_call(
        exchange,
        out_shape=[pltpu.VMEM(shape, F32) for shape in handed],
        in_specs=[hbm, hbm, hbm],
        out_specs=[vmem] * len(handed),
        scratch_shapes=[
            pltpu.VMEM((VARIANTS, PLANES, SUB, COLS), F32),
            pltpu.VMEM((VARIANTS, PLANES, SUB, COLS), F32),
            pltpu.VMEM((VARIANTS, PLANES, SUB, COLS), F32),
            pltpu.VMEM((VARIANTS, PLANES, SUB, COLS), F32),
            pltpu.VMEM((GROUPS, GROUP, PLANES, SUB, LANES), F32),
            pltpu.VMEM((GROUPS, GROUP - 1, PLANES, SUB, LANES), F32),
            pltpu.VMEM((2, 32, COLS), F32),
            pltpu.VMEM((2, 32, COLS), F32),
            pltpu.VMEM((2, 8, LANES), F32),
            pltpu.SMEM((KMAX,), jnp.int32),
            pltpu.SMEM((KMAX,), F32),
            pltpu.SMEM((BLOCKS, TILES), jnp.int32),
            dma,
            dma((GROUPS,)),
            dma,
            pltpu.SemaphoreType.REGULAR((2,)),
            dma((2,)),
            dma((2,)),
            dma((GROUPS, GROUP - 1)),
            dma((GROUPS, GROUP - 1)),
            dma((GROUPS, GROUP - 1)),
            dma((GROUPS, GROUP - 1)),
            dma((2, GROUP)),
            dma((2, GROUP)),
        ],
        compiler_params=pltpu.CompilerParams(
            collective_id=0, has_side_effects=True, vmem_limit_bytes=32 << 20),
        name="exchange",
    )(order, solute, flags)
    return pl.pallas_call(
        finish,
        out_shape=[
            jax.ShapeDtypeStruct(order.shape, F32),
            jax.ShapeDtypeStruct(solute.shape, F32),
        ],
        in_specs=[vmem] * len(handed),
        out_specs=[hbm, hbm],
        scratch_shapes=[
            pltpu.VMEM((KMAX, BV, PLANES, ROWS, COLS), F32),
            pltpu.VMEM((PLANES, ROWS, COLS), F32),
            dma((BLOCKS,)),
            dma,
        ],
        compiler_params=pltpu.CompilerParams(vmem_limit_bytes=32 << 20),
        name="finish",
    )(*results)


def solution(mesh):
    return jax.shard_map(
        shards,
        mesh=mesh,
        in_specs=(P("var", None, "space", None), P(None, "space", None), P(None, "var")),
        out_specs=(P("var", None, "space", None), P(None, "space", None)),
        check_vma=False,
    )
```

```python
import functools

import jax
import jax.numpy as jnp
from jax import lax
from jax.experimental import pallas as pl
from jax.experimental.pallas import tpu as pltpu
from jax.sharding import PartitionSpec as P

MESH = pl.DeviceIdType.MESH
F32 = jnp.float32
PLANES, ROWS, COLS, LANES = 3, 32, 1024, 128
VARIANTS, BLOCKS, BV, KMAX = 16, 8, 2, 4
SLOTS = KMAX * BV
GROUP, TILES = 8, 32
HALF = TILES // 2
SUB, GROUPS = 8, 4
PIECES = (3, 0, 1, 2)
ROUTES = ("x", "x", "direct", "y")
PEERS = ((2, 1), (1, 1), (3, 1), (2, 0), (0, 1), (1, 0), (3, 0))


def tile_blocks(active_ref, tile):
    flags = [active_ref[b, tile] for b in range(BLOCKS)]
    blocks = [jnp.int32(0)] * KMAX
    rank = jnp.int32(0)
    for b in range(BLOCKS):
        for k in range(KMAX):
            hit = jnp.where(rank == k, flags[b], 0)
            blocks[k] = blocks[k] + b * hit
        rank = rank + flags[b]
    weights = [jnp.where(rank > k, 1.0, 0.0).astype(F32) for k in range(KMAX)]
    return blocks, weights


def rows_sum(value):
    row = lax.broadcasted_iota(jnp.int32, value.shape, 0)
    before = jnp.where(row == 0, 0.0, pltpu.roll(value, 1, 0))
    after = jnp.where(row == value.shape[0] - 1, 0.0, pltpu.roll(value, value.shape[0] - 1, 0))
    return before + after


def cells_sum(value):
    return pltpu.roll(value, 1, 1) + pltpu.roll(value, value.shape[1] - 1, 1)


def plane_sum(planes, z):
    return planes[min(z + 1, PLANES - 1)] + planes[max(z - 1, 0)]


def bulk(value):
    middle = value - 0.5
    shifted = value - 0.05
    gap = value - 0.95
    return (-2.0 * middle + 9.88 * middle * middle * middle
            + 2.0 * shifted * shifted * shifted + 2.0 * gap * gap * gap)


def exchange(order, solute, active_hbm, base, slope, squares, quiet, held, edge_quiet, edge_held, edge_squares,
             blank, code,
             field0, field1, field2, field3, part, landed, row_out, row_in, edge_out,
             picked, scale, active, active_sem, load_sem, solute_sem, near_sem, row_send, row_recv,
             sum_send, sum_recv, all_send, all_recv, edge_send, edge_recv):
    v, tile = lax.axis_index("var"), lax.axis_index("space")
    x, y = v // 2, v % 2
    below, above = lax.rem(tile + TILES - 1, TILES), lax.rem(tile + 1, TILES)
    sides = (below, above)
    peers = [lax.rem(x + dx, 4) * 2 + (y + dy - 2 * y * dy) for dx, dy in PEERS]
    fields = (field0, field1, field2, field3)

    active_load = pltpu.make_async_copy(active_hbm, active, active_sem)
    active_load.start()
    loads = {}
    for g in PIECES:
        loads[g] = pltpu.make_async_copy(order.at[:, :, pl.ds(g * SUB, SUB)], fields[g], load_sem.at[g])
        loads[g].start()
    solute_load = pltpu.make_async_copy(solute, held, solute_sem)
    solute_load.start()

    first = jnp.where(lax.rem(tile, HALF) == 0, 1, 0)
    last = jnp.where(lax.rem(tile, HALF) == HALF - 1, 1, 0)

    def report(semaphore, side):
        for d in range(GROUP):
            pl.semaphore_signal(semaphore, inc=1, device_id=(lax.rem(v + d, GROUP), side), device_id_type=MESH)

    barrier = pltpu.get_barrier_semaphore()
    for peer in peers:
        pl.semaphore_signal(barrier, inc=1, device_id=(peer, tile), device_id_type=MESH)
    pl.when(last == 0)(lambda: report(barrier, above))
    pl.when(first == 1)(lambda: report(barrier, below))

    active_load.wait()
    blocks, weights = tile_blocks(active, tile)
    for k in range(KMAX):
        picked[k] = blocks[k]
        scale[k] = weights[k]
    side_blocks = [tile_blocks(active, side)[0] for side in sides]

    sums = {}
    gathers, arrived, row_copies = {}, set(), []

    def send_sums(g):
        loads[g].wait()
        for z in range(PLANES):
            total = jnp.zeros((SUB, COLS), F32)
            for k in range(KMAX):
                for i in range(BV):
                    one = fields[g][blocks[k] * BV + i, z]
                    total = total + one * one * weights[k]
            for p in range(GROUP):
                part[g, p, z] = total[:, p * LANES:(p + 1) * LANES]
        if g == PIECES[0]:
            pl.semaphore_wait(barrier, GROUP - 1 + GROUP * (1 - first + last))
        for d, peer in enumerate(peers):
            sums[g, d] = pltpu.make_async_remote_copy(
                part.at[g, peer], landed.at[g, d], sum_send.at[g, d], sum_recv.at[g, d],
                device_id=(peer, tile), device_id_type=MESH)
            sums[g, d].start()

    def stage_rows(s):
        g, edge = (0, 0) if s == 0 else (GROUPS - 1, SUB - 1)
        for k in range(KMAX):
            block = side_blocks[s][k]
            weight = active[block, tile].astype(F32)
            for i in range(BV):
                slot = k * BV + i
                for z in range(PLANES):
                    row_out[s, z * SLOTS + slot:z * SLOTS + slot + 1, :] = (
                        fields[g][block * BV + i, z, edge:edge + 1, :] * weight)
        first = 0 if s == 0 else ROWS - 2
        for z in range(PLANES):
            row_out[s, 24 + 2 * z:26 + 2 * z, :] = held[z, first:first + 2, :]
        row_out[s, 30:32, :] = jnp.zeros((2, COLS), F32)
        row_copies.append(pltpu.make_async_remote_copy(
            row_out.at[s], row_in.at[1 - s], row_send.at[s], row_recv.at[1 - s],
            device_id=(v, sides[s]), device_id_type=MESH))

    def local(k, carry):
        for i in range(BV):
            slot = k * BV + i
            weight = scale[k]
            ones = [jnp.concatenate([field[picked[k] * BV + i, z] for field in fields], axis=0)
                    for z in range(PLANES)]
            for z in range(PLANES):
                one = ones[z]
                shifted = held[z] - 0.05
                near = rows_sum(one) + cells_sum(one) + plane_sum(ones, z)
                value = one * (0.88 + 0.005 * (shifted * shifted) - 0.006 * (one * one)) + 0.02 * near
                base[slot, z] = value * weight
                slope[slot, z] = one * (0.004 * weight)
        return carry

    def gather(g, d, chunk, peer):
        gathers[g, d] = pltpu.make_async_remote_copy(
            squares.at[g, chunk], squares.at[g, chunk], all_send.at[g, d], all_recv.at[g, d],
            device_id=(peer, tile), device_id_type=MESH)
        gathers[g, d].start()

    def arrive(g, d):
        gathers[g, d].wait_recv()
        arrived.add((g, d))

    def forward(g):
        flip = PEERS.index((0, 1))
        if ROUTES[g] == "y":
            arrive(g, flip)
        for dx in (2, 1, 3):
            if ROUTES[g] == "y":
                gather(g, PEERS.index((dx, 1)), peers[flip], peers[PEERS.index((dx, 0))])
            elif ROUTES[g] == "x":
                arrive(g, PEERS.index((dx, 0)))
                gather(g, PEERS.index((dx, 1)), lax.rem(x + 4 - dx, 4) * 2 + y, peers[flip])

    def reduce(g):
        total = part[g, v]
        for d in range(GROUP - 1):
            sums[g, d].wait_recv()
            total = total + landed[g, d]
        squares[g, v] = total
        for d, (dx, dy) in enumerate(PEERS):
            if ROUTES[g] == "direct" or dx == 0 or dy == 0:
                gather(g, d, v, peers[d])
        if g in (0, GROUPS - 1):
            s, edge = (0, 0) if g == 0 else (1, SUB - 1)
            for z in range(PLANES):
                edge_out[s, z:z + 1, :] = total[z, edge:edge + 1, :]

    def start(copies):
        for copy in copies:
            copy.start()

    edges = [
        [pltpu.make_async_remote_copy(
            edge_out.at[s, 0:PLANES], edge_squares.at[1 - s, v, 0:PLANES], edge_send.at[s, d], edge_recv.at[1 - s, d],
            device_id=(lax.rem(v + d, GROUP), sides[s]), device_id_type=MESH) for d in range(GROUP)]
        for s in range(2)
    ]

    for g in PIECES:
        send_sums(g)
        if g == PIECES[0]:
            pl.when(first == 0)(lambda: report(near_sem.at[1], below))
            pl.when(last == 1)(lambda: report(near_sem.at[0], above))
    solute_load.wait()
    stage_rows(0)
    stage_rows(1)

    pl.when(last == 0)(lambda: pl.semaphore_wait(near_sem.at[1], GROUP))
    row_copies[1].start()
    pl.when(first == 0)(lambda: row_copies[0].start())
    blank[...] = jnp.zeros(blank.shape, F32)
    bits = jnp.int32(0)
    for b in range(BLOCKS):
        bits = bits + active[b, tile] * (1 << b)
    code[...] = jnp.full(code.shape, bits.astype(F32), F32)
    lax.fori_loop(0, 1, local, 0)
    reduce(PIECES[0])
    start(edges[1])
    reduce(PIECES[1])
    pl.when(first == 0)(lambda: start(edges[0]))
    reduce(PIECES[2])
    forward(PIECES[0])
    reduce(PIECES[3])
    forward(PIECES[1])

    @pl.when(first == 1)
    def _():
        pl.semaphore_wait(near_sem.at[0], GROUP)
        start(edges[0])
        row_copies[0].start()

    lax.fori_loop(1, 2, local, 0)
    forward(PIECES[2])
    lax.fori_loop(2, 4, local, 0)

    solutes = [held[z] for z in range(PLANES)]
    for z in range(PLANES):
        value = solutes[z]
        quiet[z] = bulk(value) + 6.0 * value - rows_sum(value) - cells_sum(value) - plane_sum(solutes, z)

    for copy in row_copies:
        copy.wait_recv()
    for s in range(2):
        row = 0 if s == 0 else ROWS - 1
        for k in range(KMAX):
            for i in range(BV):
                slot = k * BV + i
                for z in range(PLANES):
                    base[slot, z, row:row + 1, :] = base[slot, z, row:row + 1, :] + (
                        row_in[s, z * SLOTS + slot:z * SLOTS + slot + 1, :] * (0.02 * weights[k]))
        near_row, far_row = (1, 0) if s == 0 else (0, 1)
        nears = [row_in[s, 24 + 2 * z + near_row:25 + 2 * z + near_row, :] for z in range(PLANES)]
        for z in range(PLANES):
            far = row_in[s, 24 + 2 * z + far_row:25 + 2 * z + far_row, :]
            quiet[z, row:row + 1, :] = quiet[z, row:row + 1, :] - nears[z]
            around = far + held[z, row:row + 1, :] + cells_sum(nears[z]) + plane_sum(nears, z)
            edge_quiet[s, z:z + 1, :] = bulk(nears[z]) + 6.0 * nears[z] - around
            edge_held[s, z:z + 1, :] = nears[z]

    edges = edges[0] + edges[1]
    for place in gathers:
        if place not in arrived:
            gathers[place].wait_recv()
    for copy in edges:
        copy.wait_recv()
    for copy in list(sums.values()) + list(gathers.values()) + edges + row_copies:
        copy.wait_send()


def finish(base, slope, squares, quiet, held, edge_quiet, edge_held, edge_squares, blank, code, new_order, new_solute,
           stage, solute_stage, order_sem, solute_sem):
    bits = jnp.max(code[...]).astype(jnp.int32)

    def flag_of(b):
        return lax.bitwise_and(lax.shift_right_logical(bits, b), 1)

    def clear(b, carry):
        @pl.when(flag_of(b) == 0)
        def _():
            pltpu.make_async_copy(blank, new_order.at[pl.ds(b * BV, BV)], order_sem.at[b]).start()
        return carry

    lax.fori_loop(0, BLOCKS, clear, 0)
    totals = [
        jnp.concatenate(
            [jnp.concatenate([squares[g, p, z] for p in range(GROUP)], axis=1) for g in range(GROUPS)], axis=0)
        for z in range(PLANES)
    ]

    def update(b, rank):
        flag = flag_of(b)

        @pl.when(flag != 0)
        def _():
            for i in range(BV):
                for z in range(PLANES):
                    stage[rank, i, z] = base[rank * BV + i, z] - slope[rank * BV + i, z] * totals[z]
            pltpu.make_async_copy(stage.at[rank], new_order.at[pl.ds(b * BV, BV)], order_sem.at[b]).start()
        return rank + flag

    lax.fori_loop(0, BLOCKS, update, jnp.int32(0))
    pots = []
    for z in range(PLANES):
        pots.append(quiet[z] - 0.5 * (held[z] - 0.05) * totals[z])
    ends = []
    for s in range(2):
        total = jnp.concatenate([edge_squares[s, p, 0:PLANES] for p in range(GROUP)], axis=1)
        ends.append(edge_quiet[s, 0:PLANES] - 0.5 * (edge_held[s, 0:PLANES] - 0.05) * total)
    row = lax.broadcasted_iota(jnp.int32, (ROWS, COLS), 0)
    for z in range(PLANES):
        value = pots[z]
        before = jnp.where(row == 0, jnp.broadcast_to(ends[0][z:z + 1, :], (ROWS, COLS)), pltpu.roll(value, 1, 0))
        after = jnp.where(row == ROWS - 1, jnp.broadcast_to(ends[1][z:z + 1, :], (ROWS, COLS)),
                          pltpu.roll(value, ROWS - 1, 0))
        lap = before + after + cells_sum(value) + plane_sum(pots, z) - 6.0 * value
        solute_stage[z] = held[z] + 0.01 * lap
    out = pltpu.make_async_copy(solute_stage, new_solute, solute_sem)
    out.start()
    for b in range(BLOCKS):
        pltpu.make_async_copy(blank, new_order.at[pl.ds(b * BV, BV)], order_sem.at[b]).wait()
    out.wait()


def shards(order, solute, active):
    vmem = pl.BlockSpec(memory_space=pltpu.VMEM)
    hbm = pl.BlockSpec(memory_space=pltpu.HBM)
    dma = pltpu.SemaphoreType.DMA
    handed = [
        (SLOTS, PLANES, ROWS, COLS),
        (SLOTS, PLANES, ROWS, COLS),
        (GROUPS, GROUP, PLANES, SUB, LANES),
        (PLANES, ROWS, COLS),
        (PLANES, ROWS, COLS),
        (2, 8, COLS),
        (2, 8, COLS),
        (2, GROUP, 8, LANES),
        (BV, PLANES, ROWS, COLS),
        (8, LANES),
    ]
    order, solute, flags = (
        pltpu.with_memory_space_constraint(value, pltpu.HBM) for value in (order, solute, active.T))
    results = pl.pallas_call(
        exchange,
        out_shape=[pltpu.VMEM(shape, F32) for shape in handed],
        in_specs=[hbm, hbm, hbm],
        out_specs=[vmem] * len(handed),
        scratch_shapes=[
            pltpu.VMEM((VARIANTS, PLANES, SUB, COLS), F32),
            pltpu.VMEM((VARIANTS, PLANES, SUB, COLS), F32),
            pltpu.VMEM((VARIANTS, PLANES, SUB, COLS), F32),
            pltpu.VMEM((VARIANTS, PLANES, SUB, COLS), F32),
            pltpu.VMEM((GROUPS, GROUP, PLANES, SUB, LANES), F32),
            pltpu.VMEM((GROUPS, GROUP - 1, PLANES, SUB, LANES), F32),
            pltpu.VMEM((2, 32, COLS), F32),
            pltpu.VMEM((2, 32, COLS), F32),
            pltpu.VMEM((2, 8, LANES), F32),
            pltpu.SMEM((KMAX,), jnp.int32),
            pltpu.SMEM((KMAX,), F32),
            pltpu.SMEM((BLOCKS, TILES), jnp.int32),
            dma,
            dma((GROUPS,)),
            dma,
            pltpu.SemaphoreType.REGULAR((2,)),
            dma((2,)),
            dma((2,)),
            dma((GROUPS, GROUP - 1)),
            dma((GROUPS, GROUP - 1)),
            dma((GROUPS, GROUP - 1)),
            dma((GROUPS, GROUP - 1)),
            dma((2, GROUP)),
            dma((2, GROUP)),
        ],
        compiler_params=pltpu.CompilerParams(
            collective_id=0, has_side_effects=True, vmem_limit_bytes=32 << 20),
        name="exchange",
    )(order, solute, flags)
    return pl.pallas_call(
        finish,
        out_shape=[
            jax.ShapeDtypeStruct(order.shape, F32),
            jax.ShapeDtypeStruct(solute.shape, F32),
        ],
        in_specs=[vmem] * len(handed),
        out_specs=[hbm, hbm],
        scratch_shapes=[
            pltpu.VMEM((KMAX, BV, PLANES, ROWS, COLS), F32),
            pltpu.VMEM((PLANES, ROWS, COLS), F32),
            dma((BLOCKS,)),
            dma,
        ],
        compiler_params=pltpu.CompilerParams(vmem_limit_bytes=32 << 20),
        name="finish",
    )(*results)


def solution(mesh):
    return jax.shard_map(
        shards,
        mesh=mesh,
        in_specs=(P("var", None, "space", None), P(None, "space", None), P(None, "var")),
        out_specs=(P("var", None, "space", None), P(None, "space", None)),
        check_vma=False,
    )
```
